512 devices in a mesh: group: 16 (over z_lo, x, core), blk: 32 (over y, z_hi).
Axes of the slice: x: 4, y: 8, z: 8 (z_hi: 4, z_lo: 2; z = z_hi * 2 + z_lo), core: 2. Of those that a mesh axis runs over, the one named last changes fastest.
Arguments:
- pre_img: bfloat16 [196608, 768], P(('group', 'blk')), may hold values from -6 to 6
- pre_txt: bfloat16 [196608, 768], P(('group', 'blk')), may hold values from -6 to 6
Outputs:
- grad_img: float32 [196608, 768], P(('group', 'blk'))
- grad_txt: float32 [196608, 768], P(('group', 'blk'))
- row_loss: float32 [196608], P(('group', 'blk'))
The draws below stay inside these ranges and needn't reach their ends.
All inputs are finite; a program needn't handle non-finite values.
Results may differ from the reference program's by a relative error of at most 0.0069.
Values may be sent and summed in bfloat16 or wider, within the bound.
No kernel may reach another device: no remote copies, remote signals or barrier semaphores. Data moves between devices by JAX's collectives and lax.ppermute only.
A program may use at most 64 MiB of HBM per device.

```python
import jax
import jax.numpy as jnp
from jax import lax

E = 768
ROWS = 384
HOPS = 4
TOTAL = 196608
N_GROUP = 16
N_BLK = 32


def draw_pre_img(key, part):
    key = jax.random.fold_in(key, 1)
    return jnp.clip(jax.random.normal(key, (TOTAL, E), jnp.float32), -6.0, 6.0).astype(jnp.bfloat16)


def draw_pre_txt(key, part):
    key = jax.random.fold_in(key, 2)
    return jnp.clip(jax.random.normal(key, (TOTAL, E), jnp.float32), -6.0, 6.0).astype(jnp.bfloat16)


def setup_inputs(seed: int = 0) -> dict:
    key_list = jax.random.split(jax.random.key(seed), 3)
    pre_img = draw_pre_img(jax.random.fold_in(key_list[2], 71), 0)
    pre_txt = draw_pre_txt(jax.random.fold_in(key_list[2], 71), 0)
    return dict(pre_img=pre_img, pre_txt=pre_txt)


logit_scale = 0.32


def reference(pre_img, pre_txt):
    group_count = N_GROUP
    block_count = N_BLK
    img_soft = jnp.tanh(pre_img.astype(jnp.float32))
    txt_soft = jnp.tanh(pre_txt.astype(jnp.float32))
    images = img_soft.astype(jnp.bfloat16).reshape(group_count, block_count, ROWS, E)
    texts = txt_soft.astype(jnp.bfloat16).reshape(group_count, block_count, ROWS, E)
    eye_mask = (jnp.arange(ROWS)[:, None] == jnp.arange(ROWS)[None, :]).astype(jnp.float32)
    offsets = jnp.arange(HOPS + 1).astype(jnp.int32)
    first_mask = (jnp.arange(HOPS + 2) == 0).astype(jnp.float32)[:, None, None] * eye_mask[None]

    def forward(device):
        g_pos = device // block_count
        b_pos = device % block_count
        cycle = texts[g_pos, (b_pos - offsets) % block_count]
        hop_block = texts[(g_pos - 1) % group_count, b_pos][None]
        window = jnp.concatenate([cycle, hop_block], 0).astype(jnp.float32)
        rows_now = images[g_pos, b_pos].astype(jnp.float32)
        scores = logit_scale * jnp.einsum("re,kce->krc", rows_now, window)
        peak_value = jnp.max(jnp.max(scores, axis=2), axis=0)
        row_total = jnp.sum(jnp.sum(jnp.exp(scores - peak_value[None, :, None]), axis=2), axis=0)
        log_total = peak_value + jnp.log(row_total)
        loss_now = log_total - jnp.sum(scores[0] * eye_mask, axis=1)
        weights = (jnp.exp(scores - log_total[None, :, None]) - first_mask).astype(jnp.bfloat16)
        row_grad = logit_scale * jnp.einsum("krc,kce->re", weights.astype(jnp.float32), window)
        return loss_now, log_total, row_grad

    loss_all, lse_all, grad_rows = lax.map(forward, jnp.arange(group_count * block_count))
    lse_all = lse_all.reshape(group_count, block_count, ROWS)

    def backward(device):
        g_pos = device // block_count
        b_pos = device % block_count
        cycle_imgs = images[g_pos, (b_pos + offsets) % block_count]
        cycle_lse = lse_all[g_pos, (b_pos + offsets) % block_count]
        hop_img = images[(g_pos + 1) % group_count, b_pos][None]
        hop_lse = lse_all[(g_pos + 1) % group_count, b_pos][None]
        sources = jnp.concatenate([cycle_imgs, hop_img], 0).astype(jnp.float32)
        source_lse = jnp.concatenate([cycle_lse, hop_lse], 0)
        own_text = texts[g_pos, b_pos].astype(jnp.float32)
        scores = logit_scale * jnp.einsum("kre,ce->krc", sources, own_text)
        weights = (jnp.exp(scores - source_lse[:, :, None]) - first_mask).astype(jnp.bfloat16)
        return logit_scale * jnp.einsum("krc,kre->ce", weights.astype(jnp.float32), sources)

    grad_cols = lax.map(backward, jnp.arange(group_count * block_count))
    grad_img = grad_rows.reshape(TOTAL, E) * (1.0 - img_soft * img_soft)
    grad_txt = grad_cols.reshape(TOTAL, E) * (1.0 - txt_soft * txt_soft)
    return grad_img, grad_txt, loss_all.reshape(TOTAL)
```

```python
import jax
import jax.numpy as jnp
from jax import lax
from jax.sharding import PartitionSpec as P

logit_scale = 0.32
AXES = ("group", "blk")
LOW = -1e30


def scores_of(rows, cols):
    return logit_scale * jnp.einsum(
        "re,ce->rc", rows, cols, preferred_element_type=jnp.float32
    )


def stats_of(scores):
    peak = jnp.max(scores, axis=1)
    return peak, jnp.sum(jnp.exp(scores - peak[:, None]), axis=1)


def merge(first, second):
    peak = jnp.maximum(first[0], second[0])
    total = first[1] * jnp.exp(first[0] - peak) + second[1] * jnp.exp(second[0] - peak)
    return peak, total


def soft(scores, offset):
    return jnp.exp(scores - offset[:, None])


def dot(weights, cols):
    return jnp.dot(
        weights.astype(jnp.bfloat16), cols, preferred_element_type=jnp.float32
    )


def dot_t(weights, rows):
    return jnp.einsum(
        "rc,re->ce", weights.astype(jnp.bfloat16), rows, preferred_element_type=jnp.float32
    )


def solution(mesh):
    groups, blks = mesh.shape["group"], mesh.shape["blk"]

    def even(g, b):
        return (g + b) % 2 == 0

    def pairs(move):
        out = []
        for g in range(groups):
            for b in range(blks):
                to_g, to_b = move(g, b)
                out.append((g * blks + b, (to_g % groups) * blks + to_b % blks))
        return out

    swap = pairs(lambda g, b: (g, b + 1 if even(g, b) else b - 1))
    cross = pairs(lambda g, b: (g, b - 1 if even(g, b) else b - 3))
    uncross = [(t, s) for s, t in cross]
    back = pairs(lambda g, b: (g, b - 4))
    forth = [(t, s) for s, t in back]
    hop = pairs(lambda g, b: (g + 1, b))
    unhop = [(t, s) for s, t in hop]

    def send(array, plan):
        return lax.ppermute(array, AXES, plan)

    def per_device(pre_img, pre_txt):
        is_even = (lax.axis_index("group") + lax.axis_index("blk")) % 2 == 0
        img_soft = jnp.tanh(pre_img.astype(jnp.float32))
        txt_soft = jnp.tanh(pre_txt.astype(jnp.float32))
        image = img_soft.astype(jnp.bfloat16)
        text = txt_soft.astype(jnp.bfloat16)
        rows = image.shape[0]
        eye = (
            lax.broadcasted_iota(jnp.int32, (rows, rows), 0)
            == lax.broadcasted_iota(jnp.int32, (rows, rows), 1)
        ).astype(jnp.float32)

        text_p = send(text, swap)
        image_x = send(image, cross)
        image_v = send(image, back)
        text_h = send(text, hop)

        s_own = scores_of(image, text)
        s_vt = scores_of(image_v, text)
        s_hop = scores_of(image, text_h)
        s_xt = scores_of(image_x, text)
        s_xp = scores_of(image_x, text_p)
        image_y = jnp.where(is_even, image_v, image)
        s_yp = scores_of(image_y, text_p)

        stat_x = merge(stats_of(s_xt), stats_of(s_xp))
        stat_y = stats_of(s_yp)
        stat_v = merge(
            stats_of(s_vt),
            (jnp.where(is_even, stat_y[0], LOW), jnp.where(is_even, stat_y[1], 0.0)),
        )
        stat_i = merge(stats_of(s_own), stats_of(s_hop))
        stat_i = merge(
            stat_i,
            (jnp.where(is_even, LOW, stat_y[0]), jnp.where(is_even, 0.0, stat_y[1])),
        )
        got_x = send(jnp.stack(stat_x), uncross)
        got_v = send(jnp.stack(stat_v), forth)

        grad_y = dot(soft(s_yp, stat_y[0]), text_p)
        part_x = dot(soft(s_xt, stat_x[0]), text) + dot(soft(s_xp, stat_x[0]), text_p)
        scale_y = jnp.where(is_even, jnp.exp(stat_y[0] - stat_v[0]), 0.0)
        part_v = dot(soft(s_vt, stat_v[0]), text) + grad_y * scale_y[:, None]
        home_x = send(part_x.astype(jnp.bfloat16), uncross)
        home_v = send(part_v.astype(jnp.bfloat16), forth)

        peak, total = merge(merge(stat_i, (got_x[0], got_x[1])), (got_v[0], got_v[1]))
        lse = peak + jnp.log(total)
        lse_x = send(lse, cross)
        lse_v = send(lse, back)
        row_loss = lse - jnp.sum(s_own * eye, axis=1)

        lse_y = jnp.where(is_even, lse_v, lse)
        w_hop = soft(s_hop, lse)
        w_own = soft(s_own, lse) - eye
        term_p = dot_t(soft(s_xp, lse_x), image_x) + dot_t(soft(s_yp, lse_y), image_y)
        got_p = send(term_p.astype(jnp.bfloat16), swap)
        got_h = send(dot_t(w_hop, image).astype(jnp.bfloat16), unhop)

        scale_o = jnp.where(is_even, 0.0, jnp.exp(jnp.minimum(stat_y[0] - lse, 0.0)))
        row_grad = (
            dot(w_own, text)
            + dot(w_hop, text_h)
            + grad_y * scale_o[:, None]
            + home_x.astype(jnp.float32) * jnp.exp(got_x[0] - lse)[:, None]
            + home_v.astype(jnp.float32) * jnp.exp(got_v[0] - lse)[:, None]
        )
        text_grad = (
            dot_t(w_own, image)
            + dot_t(soft(s_vt, lse_v), image_v)
            + dot_t(soft(s_xt, lse_x), image_x)
            + got_p.astype(jnp.float32)
            + got_h.astype(jnp.float32)
        )
        grad_img = logit_scale * row_grad * (1.0 - img_soft * img_soft)
        grad_txt = logit_scale * text_grad * (1.0 - txt_soft * txt_soft)
        return grad_img, grad_txt, row_loss

    in_specs = (P(AXES, None), P(AXES, None))
    out_specs = (P(AXES, None), P(AXES, None), P(AXES))
    return jax.shard_map(
        per_device, mesh=mesh, in_specs=in_specs, out_specs=out_specs, check_vma=False
    )
```

```python
import jax
import jax.numpy as jnp
from jax import lax
from jax.experimental import pallas as pl
from jax.experimental.pallas import tpu as pltpu
from jax.sharding import PartitionSpec as P

logit_scale = 0.32
AXES = ("group", "blk")
LOW = -1e30
TAIL = 16
LIMIT = 6 << 20
F32 = jnp.float32
BF16 = jnp.bfloat16


def scores_t(text, image):
    return logit_scale * lax.dot_general(
        text, image, (((1,), (1,)), ((), ())), preferred_element_type=F32
    )


def image_term(weights_t, text):
    return lax.dot_general(
        weights_t.astype(BF16), text, (((0,), (0,)), ((), ())), preferred_element_type=F32
    )


def text_term(weights_t, image):
    return jnp.dot(weights_t.astype(BF16), image, preferred_element_type=F32)


def soft_of(pre):
    return jnp.tanh(pre[...].astype(F32))


def peak_of(*blocks):
    peak = jnp.max(blocks[0], axis=0, keepdims=True)
    for block in blocks[1:]:
        peak = jnp.maximum(peak, jnp.max(block, axis=0, keepdims=True))
    return peak


def total_of(weights):
    return jnp.sum(weights, axis=0, keepdims=True)


def merge(first, second):
    peak = jnp.maximum(first[0], second[0])
    total = first[1] * jnp.exp(first[0] - peak) + second[1] * jnp.exp(second[0] - peak)
    return peak, total


def close(first, second, third):
    peak, total = merge(merge(first, second), third)
    return peak + jnp.log(total)


def column(row):
    wide = jnp.broadcast_to(row, (128, row.shape[1]))
    return jnp.transpose(wide)[:, :1]


def pair(ref, at=0):
    return ref[at : at + 1, :], ref[at + 1 : at + 2, :]


def pack(out, part, stats):
    rows, width = part.shape
    out[:rows, :] = part.astype(BF16)
    place = lax.broadcasted_iota(jnp.int32, (TAIL, rows), 0)
    tail = jnp.zeros((TAIL, rows), F32)
    spot = 0
    for stat in stats:
        for _ in range(3):
            piece = stat.astype(BF16).astype(F32)
            tail = jnp.where(place == spot, piece, tail)
            stat = stat - piece
            spot += 1
    out[rows:, :rows] = tail.astype(BF16)
    out[rows:, rows:] = jnp.zeros((TAIL, width - rows), BF16)


def unpack(tail, spot, rows):
    tail = tail[:, :rows].astype(F32)

    def row(at):
        return tail[at : at + 1] + tail[at + 1 : at + 2] + tail[at + 2 : at + 3]

    return row(6 * spot), row(6 * spot + 3)


def hop_kernel(text, pre_hop, image_h, s_h, packed):
    image = soft_of(pre_hop).astype(BF16)
    image_h[...] = image
    scores = scores_t(text[...], image)
    s_h[...] = scores
    peak = peak_of(scores)
    weights = jnp.exp(scores - peak)
    pack(packed, image_term(weights, text[...]), (peak, total_of(weights)))


def soft_kernel(pre_img, pre_txt, image, text):
    image[...] = soft_of(pre_img).astype(BF16)
    text[...] = soft_of(pre_txt).astype(BF16)


def early_kernel(
    even, image, text, pre_p, pre_v,
    text_p, image_v, s_own, s_v, s_y, stat_v, stat_o, packed,
):
    is_even = even[0] == 1
    img = image[...]
    txt = text[...]
    other = soft_of(pre_p).astype(BF16)
    img_v = soft_of(pre_v).astype(BF16)
    text_p[...] = other
    image_v[...] = img_v
    sv = scores_t(txt, img_v)
    s_v[...] = sv
    sy = scores_t(other, jnp.where(is_even, img_v, img))
    s_y[...] = sy
    sy_v = jnp.where(is_even, sy, LOW)
    peak = peak_of(sv, sy_v)
    first = jnp.exp(sv - peak)
    second = jnp.exp(sy_v - peak)
    total = total_of(first) + total_of(second)
    stat_v[0:1, :] = peak
    stat_v[1:2, :] = total
    pack(packed, image_term(first, txt) + image_term(second, other), (peak, total))
    so = scores_t(txt, img)
    s_own[...] = so
    sy_o = jnp.where(is_even, LOW, sy)
    peak = peak_of(so, sy_o)
    stat_o[0:1, :] = peak
    stat_o[1:2, :] = total_of(jnp.exp(so - peak)) + total_of(jnp.exp(sy_o - peak))


def home_kernel(stat_o, stat_x, home_h, stat_i, stat_c):
    rows = stat_o.shape[1]
    peak, total = merge(pair(stat_o), unpack(home_h[rows:, :], 0, rows))
    stat_i[0:1, :] = peak
    stat_i[1:2, :] = total
    stat_c[0:1, :] = peak
    stat_c[1:2, :] = total
    stat_c[2:4, :] = stat_x[...]


def late_kernel(image_x, text, text_p, stat_v, s_xt, s_xp, stat_x, packed):
    img = image_x[...]
    first = scores_t(text[...], img)
    second = scores_t(text_p[...], img)
    s_xt[...] = first
    s_xp[...] = second
    peak = peak_of(first, second)
    first = jnp.exp(first - peak)
    second = jnp.exp(second - peak)
    total = total_of(first) + total_of(second)
    part = image_term(first, text[...]) + image_term(second, text_p[...])
    pack(packed, part, (peak, total) + pair(stat_v))
    stat_x[0:1, :] = peak
    stat_x[1:2, :] = total


def lse_kernel(
    even, stat_c, stat_v, from_i, from_u, home_x, home_v,
    s_xp, s_y, image_x, image_v, image, term_p, lse_i, lse_xv,
):
    is_even = even[0] == 1
    rows = stat_c.shape[1]
    tail_c, tail_v = home_x[rows:, :], home_v[rows:, :]
    own = close(pair(stat_c), unpack(tail_c, 0, rows), unpack(tail_v, 0, rows))
    of_x = close(pair(from_u), pair(stat_c, 2), unpack(tail_c, 1, rows))
    of_v = close(pair(from_i), pair(from_u, 2), pair(stat_v))
    lse_i[...] = own
    lse_xv[0:1, :] = of_x
    lse_xv[1:2, :] = of_v
    of_y = jnp.where(is_even, of_v, own)
    img_y = jnp.where(is_even, image_v[...], image[...])
    term = text_term(jnp.exp(s_xp[...] - of_x), image_x[...])
    term_p[...] = (term + text_term(jnp.exp(s_y[...] - of_y), img_y)).astype(BF16)


def image_kernel(
    even, pre_img, lse_i, s_own, s_y, text, text_p, home_x, home_v, home_h,
    grad_img, row_loss,
):
    is_even = even[0] == 1
    rows = text.shape[0]
    lse = lse_i[...]
    so = s_own[...]
    eye = lax.broadcasted_iota(jnp.int32, so.shape, 0) == lax.broadcasted_iota(
        jnp.int32, so.shape, 1
    )
    row_loss[...] = lse - jnp.sum(jnp.where(eye, so, 0.0), axis=0, keepdims=True)
    grad = image_term(jnp.exp(so - lse) - eye.astype(F32), text[...])
    sy = jnp.where(is_even, LOW, s_y[...])
    grad += image_term(jnp.exp(sy - lse), text_p[...])
    for home in (home_x, home_v, home_h):
        peak, _ = unpack(home[rows:, :], 0, rows)
        grad += home[:rows, :].astype(F32) * column(jnp.exp(peak - lse))
    soft = soft_of(pre_img)
    grad_img[...] = logit_scale * grad * (1.0 - soft * soft)


def text_kernel(
    pre_txt, lse_i, lse_xv, s_own, s_v, s_xt, image, image_v, image_x, text_sum, slope, lse_out
):
    so = s_own[...]
    eye = lax.broadcasted_iota(jnp.int32, so.shape, 0) == lax.broadcasted_iota(
        jnp.int32, so.shape, 1
    )
    term = text_term(jnp.exp(so - lse_i[...]) - eye.astype(F32), image[...])
    term += text_term(jnp.exp(s_xt[...] - lse_xv[0:1, :]), image_x[...])
    term += text_term(jnp.exp(s_v[...] - lse_xv[1:2, :]), image_v[...])
    text_sum[...] = term
    lse_out[...] = lse_i[...]
    soft = soft_of(pre_txt)
    slope[...] = logit_scale * (1.0 - soft * soft)


def more_kernel(text_sum, lse_h, s_h, image_h, text_all):
    text_all[...] = text_sum[...] + text_term(jnp.exp(s_h[...] - lse_h[...]), image_h[...])


def last_kernel(text_all, slope, got_p, grad_txt):
    grad_txt[...] = (text_all[...] + got_p[...].astype(F32)) * slope[...]


def together(*arrays):
    return lax.optimization_barrier(arrays)


def solution(mesh):
    groups, blks = mesh.shape["group"], mesh.shape["blk"]

    def even_at(g, b):
        return (g + b) % 2 == 0

    def pairs(move):
        out = []
        for g in range(groups):
            for b in range(blks):
                to_g, to_b = move(g, b)
                out.append((g * blks + b, (to_g % groups) * blks + to_b % blks))
        return out

    swap = pairs(lambda g, b: (g, b + 1 if even_at(g, b) else b - 1))
    cross = pairs(lambda g, b: (g, b - 1 if even_at(g, b) else b - 3))
    uncross = [(t, s) for s, t in cross]
    back = pairs(lambda g, b: (g, b - 4))
    forth = [(t, s) for s, t in back]
    unhop = pairs(lambda g, b: (g - 1, b))
    hop = [(t, s) for s, t in unhop]

    def send(array, plan):
        return lax.ppermute(array, AXES, plan)

    def run(kernel, outs, *args, matmuls=0, name=None):
        vmem = pl.BlockSpec(memory_space=pltpu.VMEM)
        smem = pl.BlockSpec(memory_space=pltpu.SMEM)
        return pl.pallas_call(
            kernel,
            out_shape=outs,
            in_specs=[smem if v.dtype == jnp.int32 else vmem for v in args],
            out_specs=[vmem] * len(outs),
            compiler_params=pltpu.CompilerParams(vmem_limit_bytes=LIMIT),
            cost_estimate=pl.CostEstimate(
                flops=matmuls * 2 * 384 * 384 * 768, bytes_accessed=0, transcendentals=0
            ),
            name=name,
        )(*args)

    def per_device(pre_img, pre_txt):
        rows, width = pre_img.shape
        block = jax.ShapeDtypeStruct((rows, width), BF16)
        packed = jax.ShapeDtypeStruct((rows + TAIL, width), BF16)
        wide = jax.ShapeDtypeStruct((rows, width), F32)
        square = jax.ShapeDtypeStruct((rows, rows), F32)

        def stat(count):
            return jax.ShapeDtypeStruct((count, rows), F32)

        even = (lax.axis_index("group") + lax.axis_index("blk")) % 2 == 0
        even = even.astype(jnp.int32).reshape(1)

        pre_h = send(pre_img, unhop)
        pre_v = send(pre_img, back)
        pre_p = send(pre_txt, swap)
        image, text = run(soft_kernel, (block, block), pre_img, pre_txt, name="soft")
        pre_p, img_x = together(pre_p, image)
        image_x = send(img_x, cross)

        text_p, image_v, s_own, s_v, s_y, stat_v, stat_o, part_v = run(
            early_kernel,
            (block, block, square, square, square, stat(2), stat(2), packed),
            even, image, text, pre_p, pre_v, matmuls=5, name="early",
        )
        home_v = send(part_v, forth)
        text_p, pre_h = together(text_p, pre_h)
        image_h, s_h, part_h = run(
            hop_kernel, (block, square, packed), text, pre_h, matmuls=2, name="hop"
        )
        home_h = send(part_h, hop)
        s_xt, s_xp, stat_x, part_x = run(
            late_kernel,
            (square, square, stat(2), packed),
            image_x, text, text_p, stat_v, matmuls=4, name="late",
        )
        home_x = send(part_x, uncross)
        stat_i, stat_c = run(
            home_kernel, (stat(2), stat(4)), stat_o, stat_x, home_h, name="home"
        )
        from_i = send(stat_i, back)
        from_u = send(stat_c, cross)
        term_p, lse_i, lse_xv = run(
            lse_kernel,
            (block, stat(1), stat(2)),
            even, stat_c, stat_v, from_i, from_u, home_x, home_v,
            s_xp, s_y, image_x, image_v, image, matmuls=2, name="lse",
        )
        got_p = send(term_p, swap)
        grad_img, row_loss = run(
            image_kernel,
            (wide, stat(1)),
            even, pre_img, lse_i, s_own, s_y, text, text_p, home_x, home_v, home_h,
            matmuls=2, name="image",
        )
        text_sum, slope, lse_out = run(
            text_kernel,
            (wide, wide, stat(1)),
            pre_txt, lse_i, lse_xv, s_own, s_v, s_xt, image, image_v, image_x,
            matmuls=3, name="text",
        )
        lse_h = send(lse_out, unhop)
        (text_all,) = run(
            more_kernel, (wide,), text_sum, lse_h, s_h, image_h, matmuls=1, name="more"
        )
        (grad_txt,) = run(last_kernel, (wide,), text_all, slope, got_p, name="last")
        return grad_img, grad_txt, row_loss.reshape(rows)

    in_specs = (P(AXES, None), P(AXES, None))
    out_specs = (P(AXES, None), P(AXES, None), P(AXES))
    return jax.shard_map(
        per_device, mesh=mesh, in_specs=in_specs, out_specs=out_specs, check_vma=False
    )
```

```python
import jax
import jax.numpy as jnp
from jax import lax
from jax.experimental import pallas as pl
from jax.experimental.pallas import tpu as pltpu
from jax.sharding import PartitionSpec as P

logit_scale = 0.32
AXES = ("group", "blk")
LOW = -1e30
TAIL = 16
LIMIT = 6 << 20
F32 = jnp.float32
BF16 = jnp.bfloat16


def scores_t(text, image):
    return logit_scale * lax.dot_general(
        text, image, (((1,), (1,)), ((), ())), preferred_element_type=F32
    )


def image_term(weights_t, text):
    return lax.dot_general(
        weights_t.astype(BF16), text, (((0,), (0,)), ((), ())), preferred_element_type=F32
    )


def text_term(weights_t, image):
    return jnp.dot(weights_t.astype(BF16), image, preferred_element_type=F32)


def soft_of(pre):
    return jnp.tanh(pre[...].astype(F32))


def peak_of(*blocks):
    peak = jnp.max(blocks[0], axis=0, keepdims=True)
    for block in blocks[1:]:
        peak = jnp.maximum(peak, jnp.max(block, axis=0, keepdims=True))
    return peak


def total_of(weights):
    return jnp.sum(weights, axis=0, keepdims=True)


def merge(first, second):
    peak = jnp.maximum(first[0], second[0])
    total = first[1] * jnp.exp(first[0] - peak) + second[1] * jnp.exp(second[0] - peak)
    return peak, total


def close(first, second, third):
    peak, total = merge(merge(first, second), third)
    return peak + jnp.log(total)


def column(row):
    wide = jnp.broadcast_to(row, (128, row.shape[1]))
    return jnp.transpose(wide)[:, :1]


def pair(ref, at=0):
    return ref[at : at + 1, :], ref[at + 1 : at + 2, :]


def pack(out, part, stats):
    out[: part.shape[0], :] = part.astype(BF16)
    pack_tail(out, part.shape[0], stats)


def pack_tail(out, rows, stats):
    width = out.shape[1]
    place = lax.broadcasted_iota(jnp.int32, (TAIL, rows), 0)
    tail = jnp.zeros((TAIL, rows), F32)
    spot = 0
    for stat in stats:
        for _ in range(3):
            piece = stat.astype(BF16).astype(F32)
            tail = jnp.where(place == spot, piece, tail)
            stat = stat - piece
            spot += 1
    out[rows:, :rows] = tail.astype(BF16)
    out[rows:, rows:] = jnp.zeros((TAIL, width - rows), BF16)


def unpack(tail, spot, rows):
    tail = tail[:, :rows].astype(F32)

    def row(at):
        return tail[at : at + 1] + tail[at + 1 : at + 2] + tail[at + 2 : at + 3]

    return row(6 * spot), row(6 * spot + 3)


def hop_kernel(text, pre_hop, image_h, s_h, packed):
    image = soft_of(pre_hop).astype(BF16)
    image_h[...] = image
    scores = scores_t(text[...], image)
    s_h[...] = scores
    peak = peak_of(scores)
    weights = jnp.exp(scores - peak)
    pack(packed, image_term(weights, text[...]), (peak, total_of(weights)))


def soft_kernel(pre_img, pre_txt, image, text):
    image[...] = soft_of(pre_img).astype(BF16)
    text[...] = soft_of(pre_txt).astype(BF16)


def early_kernel(
    even, image, text, pre_p, pre_v,
    text_p, image_v, s_own, s_v, s_y, stat_v, stat_o, packed,
):
    is_even = even[0] == 1
    img = image[...]
    txt = text[...]
    other = soft_of(pre_p).astype(BF16)
    img_v = soft_of(pre_v).astype(BF16)
    text_p[...] = other
    image_v[...] = img_v
    sv = scores_t(txt, img_v)
    s_v[...] = sv
    sy = scores_t(other, jnp.where(is_even, img_v, img))
    s_y[...] = sy
    sy_v = jnp.where(is_even, sy, LOW)
    peak = peak_of(sv, sy_v)
    first = jnp.exp(sv - peak)
    second = jnp.exp(sy_v - peak)
    total = total_of(first) + total_of(second)
    stat_v[0:1, :] = peak
    stat_v[1:2, :] = total
    pack(packed, image_term(first, txt) + image_term(second, other), (peak, total))
    so = scores_t(txt, img)
    s_own[...] = so
    sy_o = jnp.where(is_even, LOW, sy)
    peak = peak_of(so, sy_o)
    stat_o[0:1, :] = peak
    stat_o[1:2, :] = total_of(jnp.exp(so - peak)) + total_of(jnp.exp(sy_o - peak))


def home_kernel(stat_o, stat_x, home_h, stat_i, stat_c):
    rows = stat_o.shape[1]
    peak, total = merge(pair(stat_o), unpack(home_h[rows:, :], 0, rows))
    stat_i[0:1, :] = peak
    stat_i[1:2, :] = total
    stat_c[0:1, :] = peak
    stat_c[1:2, :] = total
    stat_c[2:4, :] = stat_x[...]


def late_kernel(image_x, text, text_p, stat_v, s_xt, s_xp, stat_x, packed):
    rows = text.shape[0]
    for low, high in ((0, 256), (256, rows)):
        img = image_x[low:high, :]
        first = scores_t(text[...], img)
        second = scores_t(text_p[...], img)
        s_xt[:, low:high] = first
        s_xp[:, low:high] = second
        peak = peak_of(first, second)
        first = jnp.exp(first - peak)
        second = jnp.exp(second - peak)
        part = image_term(first, text[...]) + image_term(second, text_p[...])
        packed[low:high, :] = part.astype(BF16)
        stat_x[0:1, low:high] = peak
        stat_x[1:2, low:high] = total_of(first) + total_of(second)
    pack_tail(packed, rows, pair(stat_x) + pair(stat_v))


def lse_kernel(
    even, stat_c, stat_v, from_i, from_u, home_x, home_v,
    s_xp, s_y, image_x, image_v, image, term_p, lse_i, lse_xv,
):
    is_even = even[0] == 1
    rows = stat_c.shape[1]
    tail_c, tail_v = home_x[rows:, :], home_v[rows:, :]
    own = close(pair(stat_c), unpack(tail_c, 0, rows), unpack(tail_v, 0, rows))
    of_x = close(pair(from_u), pair(stat_c, 2), unpack(tail_c, 1, rows))
    of_v = close(pair(from_i), pair(from_u, 2), pair(stat_v))
    lse_i[...] = own
    lse_xv[0:1, :] = of_x
    lse_xv[1:2, :] = of_v
    of_y = jnp.where(is_even, of_v, own)
    img_y = jnp.where(is_even, image_v[...], image[...])
    term = text_term(jnp.exp(s_xp[...] - of_x), image_x[...])
    term_p[...] = (term + text_term(jnp.exp(s_y[...] - of_y), img_y)).astype(BF16)


def image_kernel(
    even, pre_img, lse_i, s_own, s_y, text, text_p, home_x, home_v, home_h,
    grad_img, row_loss,
):
    is_even = even[0] == 1
    rows = text.shape[0]
    lse = lse_i[...]
    so = s_own[...]
    eye = lax.broadcasted_iota(jnp.int32, so.shape, 0) == lax.broadcasted_iota(
        jnp.int32, so.shape, 1
    )
    row_loss[...] = lse - jnp.sum(jnp.where(eye, so, 0.0), axis=0, keepdims=True)
    grad = image_term(jnp.exp(so - lse) - eye.astype(F32), text[...])
    sy = jnp.where(is_even, LOW, s_y[...])
    grad += image_term(jnp.exp(sy - lse), text_p[...])
    for home in (home_x, home_v, home_h):
        peak, _ = unpack(home[rows:, :], 0, rows)
        grad += home[:rows, :].astype(F32) * column(jnp.exp(peak - lse))
    soft = soft_of(pre_img)
    grad_img[...] = logit_scale * grad * (1.0 - soft * soft)


def text_kernel(
    pre_txt, lse_i, lse_xv, s_own, s_v, s_xt, image, image_v, image_x, text_sum, slope, lse_out
):
    so = s_own[...]
    eye = lax.broadcasted_iota(jnp.int32, so.shape, 0) == lax.broadcasted_iota(
        jnp.int32, so.shape, 1
    )
    term = text_term(jnp.exp(so - lse_i[...]) - eye.astype(F32), image[...])
    term += text_term(jnp.exp(s_xt[...] - lse_xv[0:1, :]), image_x[...])
    term += text_term(jnp.exp(s_v[...] - lse_xv[1:2, :]), image_v[...])
    text_sum[...] = term
    lse_out[...] = lse_i[...]
    soft = soft_of(pre_txt)
    slope[...] = logit_scale * (1.0 - soft * soft)


def more_kernel(text_sum, lse_h, s_h, image_h, text_all):
    text_all[...] = text_sum[...] + text_term(jnp.exp(s_h[...] - lse_h[...]), image_h[...])


def together(*arrays):
    return lax.optimization_barrier(arrays)


def solution(mesh):
    groups, blks = mesh.shape["group"], mesh.shape["blk"]

    def even_at(g, b):
        return (g + b) % 2 == 0

    def pairs(move):
        out = []
        for g in range(groups):
            for b in range(blks):
                to_g, to_b = move(g, b)
                out.append((g * blks + b, (to_g % groups) * blks + to_b % blks))
        return out

    swap = pairs(lambda g, b: (g, b + 1 if even_at(g, b) else b - 1))
    cross = pairs(lambda g, b: (g, b - 1 if even_at(g, b) else b - 3))
    uncross = [(t, s) for s, t in cross]
    back = pairs(lambda g, b: (g, b - 4))
    forth = [(t, s) for s, t in back]
    unhop = pairs(lambda g, b: (g - 1, b))
    hop = [(t, s) for s, t in unhop]

    def send(array, plan):
        return lax.ppermute(array, AXES, plan)

    def run(kernel, outs, *args, matmuls=0, name=None):
        vmem = pl.BlockSpec(memory_space=pltpu.VMEM)
        smem = pl.BlockSpec(memory_space=pltpu.SMEM)
        return pl.pallas_call(
            kernel,
            out_shape=outs,
            in_specs=[smem if v.dtype == jnp.int32 else vmem for v in args],
            out_specs=[vmem] * len(outs),
            compiler_params=pltpu.CompilerParams(vmem_limit_bytes=LIMIT),
            cost_estimate=pl.CostEstimate(
                flops=matmuls * 2 * 384 * 384 * 768, bytes_accessed=0, transcendentals=0
            ),
            name=name,
        )(*args)

    def per_device(pre_img, pre_txt):
        rows, width = pre_img.shape
        block = jax.ShapeDtypeStruct((rows, width), BF16)
        packed = jax.ShapeDtypeStruct((rows + TAIL, width), BF16)
        wide = jax.ShapeDtypeStruct((rows, width), F32)
        square = jax.ShapeDtypeStruct((rows, rows), F32)

        def stat(count):
            return jax.ShapeDtypeStruct((count, rows), F32)

        even = (lax.axis_index("group") + lax.axis_index("blk")) % 2 == 0
        even = even.astype(jnp.int32).reshape(1)

        pre_h = send(pre_img, unhop)
        pre_v = send(pre_img, back)
        pre_p = send(pre_txt, swap)
        image, text = run(soft_kernel, (block, block), pre_img, pre_txt, name="soft")
        pre_p, img_x = together(pre_p, image)
        image_x = send(img_x, cross)

        text_p, image_v, s_own, s_v, s_y, stat_v, stat_o, part_v = run(
            early_kernel,
            (block, block, square, square, square, stat(2), stat(2), packed),
            even, image, text, pre_p, pre_v, matmuls=5, name="early",
        )
        home_v = send(part_v, forth)
        text_p, pre_h = together(text_p, pre_h)
        image_h, s_h, part_h = run(
            hop_kernel, (block, square, packed), text, pre_h, matmuls=2, name="hop"
        )
        home_h = send(part_h, hop)
        s_xt, s_xp, stat_x, part_x = run(
            late_kernel,
            (square, square, stat(2), packed),
            image_x, text, text_p, stat_v, matmuls=4, name="late",
        )
        home_x = send(part_x, uncross)
        stat_i, stat_c = run(
            home_kernel, (stat(2), stat(4)), stat_o, stat_x, home_h, name="home"
        )
        from_i = send(stat_i, back)
        from_u = send(stat_c, cross)
        term_p, lse_i, lse_xv = run(
            lse_kernel,
            (block, stat(1), stat(2)),
            even, stat_c, stat_v, from_i, from_u, home_x, home_v,
            s_xp, s_y, image_x, image_v, image, matmuls=2, name="lse",
        )
        got_p = send(term_p, swap)
        grad_img, row_loss = run(
            image_kernel,
            (wide, stat(1)),
            even, pre_img, lse_i, s_own, s_y, text, text_p, home_x, home_v, home_h,
            matmuls=2, name="image",
        )
        text_sum, slope, lse_out = run(
            text_kernel,
            (wide, wide, stat(1)),
            pre_txt, lse_i, lse_xv, s_own, s_v, s_xt, image, image_v, image_x,
            matmuls=3, name="text",
        )
        lse_h = send(lse_out, unhop)
        (text_all,) = run(
            more_kernel, (wide,), text_sum, lse_h, s_h, image_h, matmuls=1, name="more"
        )
        grad_txt = (text_all + got_p.astype(F32)) * slope
        return grad_img, grad_txt, row_loss.reshape(rows)

    in_specs = (P(AXES, None), P(AXES, None))
    out_specs = (P(AXES, None), P(AXES, None), P(AXES))
    return jax.shard_map(
        per_device, mesh=mesh, in_specs=in_specs, out_specs=out_specs, check_vma=False
    )
```

```python
import jax
import jax.numpy as jnp
from jax import lax
from jax.experimental import pallas as pl
from jax.experimental.pallas import tpu as pltpu
from jax.sharding import PartitionSpec as P

logit_scale = 0.32
AXES = ("group", "blk")
LOW = -1e30
TAIL = 16
LIMIT = 6 << 20
F32 = jnp.float32
BF16 = jnp.bfloat16


def scores_t(text, image):
    return logit_scale * lax.dot_general(
        text, image, (((1,), (1,)), ((), ())), preferred_element_type=F32
    )


def image_term(weights_t, text):
    return lax.dot_general(
        weights_t.astype(BF16), text, (((0,), (0,)), ((), ())), preferred_element_type=F32
    )


def text_term(weights_t, image):
    return jnp.dot(weights_t.astype(BF16), image, preferred_element_type=F32)


def soft_of(pre):
    return jnp.tanh(pre[...].astype(F32))


def peak_of(*blocks):
    peak = jnp.max(blocks[0], axis=0, keepdims=True)
    for block in blocks[1:]:
        peak = jnp.maximum(peak, jnp.max(block, axis=0, keepdims=True))
    return peak


def total_of(weights):
    return jnp.sum(weights, axis=0, keepdims=True)


def merge(first, second):
    peak = jnp.maximum(first[0], second[0])
    total = first[1] * jnp.exp(first[0] - peak) + second[1] * jnp.exp(second[0] - peak)
    return peak, total


def close(first, second, third):
    peak, total = merge(merge(first, second), third)
    return peak + jnp.log(total)


def column(row):
    wide = jnp.broadcast_to(row, (128, row.shape[1]))
    return jnp.transpose(wide)[:, :1]


def pair(ref, at=0):
    return ref[at : at + 1, :], ref[at + 1 : at + 2, :]


def pack(out, part, stats):
    rows, width = part.shape
    out[:rows, :] = part.astype(BF16)
    place = lax.broadcasted_iota(jnp.int32, (TAIL, rows), 0)
    tail = jnp.zeros((TAIL, rows), F32)
    spot = 0
    for stat in stats:
        for _ in range(3):
            piece = stat.astype(BF16).astype(F32)
            tail = jnp.where(place == spot, piece, tail)
            stat = stat - piece
            spot += 1
    out[rows:, :rows] = tail.astype(BF16)
    out[rows:, rows:] = jnp.zeros((TAIL, width - rows), BF16)


def unpack(tail, spot, rows):
    tail = tail[:, :rows].astype(F32)

    def row(at):
        return tail[at : at + 1] + tail[at + 1 : at + 2] + tail[at + 2 : at + 3]

    return row(6 * spot), row(6 * spot + 3)


def hop_kernel(even, text, image_o, s_y, pre_hop, image_h, s_h, s_own, stat_o, packed):
    image = soft_of(pre_hop).astype(BF16)
    image_h[...] = image
    scores = scores_t(text[...], image)
    s_h[...] = scores
    peak = peak_of(scores)
    weights = jnp.exp(scores - peak)
    pack(packed, image_term(weights, text[...]), (peak, total_of(weights)))
    so = scores_t(text[...], image_o[...])
    s_own[...] = so
    sy_o = jnp.where(even[0] == 1, LOW, s_y[...])
    peak = peak_of(so, sy_o)
    stat_o[0:1, :] = peak
    stat_o[1:2, :] = total_of(jnp.exp(so - peak)) + total_of(jnp.exp(sy_o - peak))


def soft_kernel(pre_img, pre_txt, image, text):
    image[...] = soft_of(pre_img).astype(BF16)
    text[...] = soft_of(pre_txt).astype(BF16)


def early_kernel(
    even, image, text, pre_p, pre_v,
    text_p, image_v, s_v, s_y, stat_v, packed,
):
    is_even = even[0] == 1
    img = image[...]
    txt = text[...]
    other = soft_of(pre_p).astype(BF16)
    img_v = soft_of(pre_v).astype(BF16)
    text_p[...] = other
    image_v[...] = img_v
    sv = scores_t(txt, img_v)
    s_v[...] = sv
    sy = scores_t(other, jnp.where(is_even, img_v, img))
    s_y[...] = sy
    sy_v = jnp.where(is_even, sy, LOW)
    peak = peak_of(sv, sy_v)
    first = jnp.exp(sv - peak)
    second = jnp.exp(sy_v - peak)
    total = total_of(first) + total_of(second)
    stat_v[0:1, :] = peak
    stat_v[1:2, :] = total
    pack(packed, image_term(first, txt) + image_term(second, other), (peak, total))


def home_kernel(stat_o, stat_x, home_h, stat_i, stat_c):
    rows = stat_o.shape[1]
    peak, total = merge(pair(stat_o), unpack(home_h[rows:, :], 0, rows))
    stat_i[0:1, :] = peak
    stat_i[1:2, :] = total
    stat_c[0:1, :] = peak
    stat_c[1:2, :] = total
    stat_c[2:4, :] = stat_x[...]


def late_kernel(image_x, text, text_p, stat_v, s_xt, s_xp, stat_x, packed):
    img = image_x[...]
    first = scores_t(text[...], img)
    second = scores_t(text_p[...], img)
    s_xt[...] = first
    s_xp[...] = second
    peak = peak_of(first, second)
    first = jnp.exp(first - peak)
    second = jnp.exp(second - peak)
    total = total_of(first) + total_of(second)
    part = image_term(first, text[...]) + image_term(second, text_p[...])
    pack(packed, part, (peak, total) + pair(stat_v))
    stat_x[0:1, :] = peak
    stat_x[1:2, :] = total


def lse_kernel(
    even, stat_c, stat_v, from_i, from_u, home_x, home_v,
    s_xp, s_y, image_x, image_v, image, term_p, lse_i, lse_xv,
):
    is_even = even[0] == 1
    rows = stat_c.shape[1]
    tail_c, tail_v = home_x[rows:, :], home_v[rows:, :]
    own = close(pair(stat_c), unpack(tail_c, 0, rows), unpack(tail_v, 0, rows))
    of_x = close(pair(from_u), pair(stat_c, 2), unpack(tail_c, 1, rows))
    of_v = close(pair(from_i), pair(from_u, 2), pair(stat_v))
    lse_i[...] = own
    lse_xv[0:1, :] = of_x
    lse_xv[1:2, :] = of_v
    of_y = jnp.where(is_even, of_v, own)
    img_y = jnp.where(is_even, image_v[...], image[...])
    term = text_term(jnp.exp(s_xp[...] - of_x), image_x[...])
    term_p[...] = (term + text_term(jnp.exp(s_y[...] - of_y), img_y)).astype(BF16)


def image_kernel(
    even, pre_img, lse_i, s_own, s_y, text, text_p, home_x, home_v, home_h,
    grad_img, row_loss,
):
    is_even = even[0] == 1
    rows = text.shape[0]
    lse = lse_i[...]
    so = s_own[...]
    eye = lax.broadcasted_iota(jnp.int32, so.shape, 0) == lax.broadcasted_iota(
        jnp.int32, so.shape, 1
    )
    row_loss[...] = lse - jnp.sum(jnp.where(eye, so, 0.0), axis=0, keepdims=True)
    grad = image_term(jnp.exp(so - lse) - eye.astype(F32), text[...])
    sy = jnp.where(is_even, LOW, s_y[...])
    grad += image_term(jnp.exp(sy - lse), text_p[...])
    for home in (home_x, home_v, home_h):
        peak, _ = unpack(home[rows:, :], 0, rows)
        grad += home[:rows, :].astype(F32) * column(jnp.exp(peak - lse))
    soft = soft_of(pre_img)
    grad_img[...] = logit_scale * grad * (1.0 - soft * soft)


def text_kernel(
    pre_txt, lse_i, lse_xv, s_own, s_v, s_xt, image, image_v, image_x, text_sum, slope, lse_out
):
    so = s_own[...]
    eye = lax.broadcasted_iota(jnp.int32, so.shape, 0) == lax.broadcasted_iota(
        jnp.int32, so.shape, 1
    )
    term = text_term(jnp.exp(so - lse_i[...]) - eye.astype(F32), image[...])
    term += text_term(jnp.exp(s_xt[...] - lse_xv[0:1, :]), image_x[...])
    term += text_term(jnp.exp(s_v[...] - lse_xv[1:2, :]), image_v[...])
    text_sum[...] = term
    lse_out[...] = lse_i[...]
    soft = soft_of(pre_txt)
    slope[...] = logit_scale * (1.0 - soft * soft)


def more_kernel(text_sum, lse_h, s_h, image_h, text_all):
    text_all[...] = text_sum[...] + text_term(jnp.exp(s_h[...] - lse_h[...]), image_h[...])


def last_kernel(text_all, slope, got_p, grad_txt):
    grad_txt[...] = (text_all[...] + got_p[...].astype(F32)) * slope[...]


def together(*arrays):
    return lax.optimization_barrier(arrays)


def solution(mesh):
    groups, blks = mesh.shape["group"], mesh.shape["blk"]

    def even_at(g, b):
        return (g + b) % 2 == 0

    def pairs(move):
        out = []
        for g in range(groups):
            for b in range(blks):
                to_g, to_b = move(g, b)
                out.append((g * blks + b, (to_g % groups) * blks + to_b % blks))
        return out

    swap = pairs(lambda g, b: (g, b + 1 if even_at(g, b) else b - 1))
    cross = pairs(lambda g, b: (g, b - 1 if even_at(g, b) else b - 3))
    uncross = [(t, s) for s, t in cross]
    back = pairs(lambda g, b: (g, b - 4))
    forth = [(t, s) for s, t in back]
    unhop = pairs(lambda g, b: (g - 1, b))
    hop = [(t, s) for s, t in unhop]

    def send(array, plan):
        return lax.ppermute(array, AXES, plan)

    def run(kernel, outs, *args, matmuls=0, name=None):
        vmem = pl.BlockSpec(memory_space=pltpu.VMEM)
        smem = pl.BlockSpec(memory_space=pltpu.SMEM)
        return pl.pallas_call(
            kernel,
            out_shape=outs,
            in_specs=[smem if v.dtype == jnp.int32 else vmem for v in args],
            out_specs=[vmem] * len(outs),
            compiler_params=pltpu.CompilerParams(vmem_limit_bytes=LIMIT),
            cost_estimate=pl.CostEstimate(
                flops=matmuls * 2 * 384 * 384 * 768, bytes_accessed=0, transcendentals=0
            ),
            name=name,
        )(*args)

    def per_device(pre_img, pre_txt):
        rows, width = pre_img.shape
        block = jax.ShapeDtypeStruct((rows, width), BF16)
        packed = jax.ShapeDtypeStruct((rows + TAIL, width), BF16)
        wide = jax.ShapeDtypeStruct((rows, width), F32)
        square = jax.ShapeDtypeStruct((rows, rows), F32)

        def stat(count):
            return jax.ShapeDtypeStruct((count, rows), F32)

        even = (lax.axis_index("group") + lax.axis_index("blk")) % 2 == 0
        even = even.astype(jnp.int32).reshape(1)

        pre_h = send(pre_img, unhop)
        pre_v = send(pre_img, back)
        pre_p = send(pre_txt, swap)
        image, text = run(soft_kernel, (block, block), pre_img, pre_txt, name="soft")
        pre_p, img_x = together(pre_p, image)
        image_x = send(img_x, cross)

        text_p, image_v, s_v, s_y, stat_v, part_v = run(
            early_kernel,
            (block, block, square, square, stat(2), packed),
            even, image, text, pre_p, pre_v, matmuls=4, name="early",
        )
        home_v = send(part_v, forth)
        text_p, pre_h = together(text_p, pre_h)
        image_h, s_h, s_own, stat_o, part_h = run(
            hop_kernel,
            (block, square, square, stat(2), packed),
            even, text, image, s_y, pre_h, matmuls=3, name="hop",
        )
        home_h = send(part_h, hop)
        s_xt, s_xp, stat_x, part_x = run(
            late_kernel,
            (square, square, stat(2), packed),
            image_x, text, text_p, stat_v, matmuls=4, name="late",
        )
        home_x = send(part_x, uncross)
        stat_i, stat_c = run(
            home_kernel, (stat(2), stat(4)), stat_o, stat_x, home_h, name="home"
        )
        from_i = send(stat_i, back)
        from_u = send(stat_c, cross)
        term_p, lse_i, lse_xv = run(
            lse_kernel,
            (block, stat(1), stat(2)),
            even, stat_c, stat_v, from_i, from_u, home_x, home_v,
            s_xp, s_y, image_x, image_v, image, matmuls=2, name="lse",
        )
        got_p = send(term_p, swap)
        grad_img, row_loss = run(
            image_kernel,
            (wide, stat(1)),
            even, pre_img, lse_i, s_own, s_y, text, text_p, home_x, home_v, home_h,
            matmuls=2, name="image",
        )
        text_sum, slope, lse_out = run(
            text_kernel,
            (wide, wide, stat(1)),
            pre_txt, lse_i, lse_xv, s_own, s_v, s_xt, image, image_v, image_x,
            matmuls=3, name="text",
        )
        lse_h = send(lse_out, unhop)
        (text_all,) = run(
            more_kernel, (wide,), text_sum, lse_h, s_h, image_h, matmuls=1, name="more"
        )
        (grad_txt,) = run(last_kernel, (wide,), text_all, slope, got_p, name="last")
        return grad_img, grad_txt, row_loss.reshape(rows)

    in_specs = (P(AXES, None), P(AXES, None))
    out_specs = (P(AXES, None), P(AXES, None), P(AXES))
    return jax.shard_map(
        per_device, mesh=mesh, in_specs=in_specs, out_specs=out_specs, check_vma=False
    )
```
